32 devices in a mesh: leg: 2 (over y), ping: 8 (over z, core), rng: 2 (over x).
Axes of the slice: x: 2, y: 2, z: 4, core: 2. Of those that a mesh axis runs over, the one named last changes fastest.
Arguments:
- echo: bfloat16 [2, 16384, 256], P(None, ('leg', 'ping'), 'rng'), parts along dimension 1, may hold values from -6 to 6
- steer: bfloat16 [2, 16384, 8192], P(None, ('leg', 'rng'), 'ping'), parts along dimension 1, may hold values from -0.046875 to 0.046875
- offsets: int32 [256], P(('leg', 'ping')), parts along dimension 0, may hold values from 0 to 15
- taps: float32 [256, 4], P(('leg', 'ping')), parts along dimension 0, may hold values from 0.1 to 1
- centers: int32 [512], P(('leg', 'ping', 'rng')), parts along dimension 0, may hold values from 0 to 8191
- halves: int32 [512], P(('leg', 'ping', 'rng')), parts along dimension 0, may hold values from 128 to 1024
Outputs:
- focused: float32 [2, 512, 8192], P(None, ('leg', 'ping', 'rng')), parts along dimension 1
- phase_error: float32 [16384], P('leg'), parts along dimension 0
The draws below stay inside these ranges and needn't reach their ends.
There are 2 independent parts, one for each index of `leg`. The reference program is written for one: setup_inputs(seed, part) draws one part's arguments, and reference() takes and returns one part's arrays. A program takes and returns all parts, laid end to end along the dimension named above; each array names one. Nothing has to cross between parts.
All inputs are finite; a program needn't handle non-finite values.
Results may differ from the reference program's by a relative error of at most 0.0049.
Values may be sent and summed in bfloat16 or wider, within the bound.
No kernel may reach another device: no remote copies, remote signals or barrier semaphores. Data moves between devices by JAX's collectives and lax.ppermute only.
A program may use at most 64 MiB of HBM per device.

```python
import math
import jax
import jax.numpy as jnp
from jax import lax

A = 8192
PBLK = 64
NTAP = 4
MAXOFF = 16
R = 256
P_SIZE = 8192
NBLK = 128


def place_ends(array, key, smallest, high):
    place = [jax.random.randint(jax.random.fold_in(key, axis), (), 0, length) for axis, length in enumerate(array.shape)]
    widest = array.shape.index(max(array.shape))
    beside = place[:widest] + [(place[widest] + 1) % array.shape[widest]] + place[widest + 1:]
    return array.at[tuple(place)].set(smallest).at[tuple(beside)].set(high)


def level_of(rng, shape, shards, low, high):
    level, own = 1.0, jax.random.fold_in(rng, 6)
    for axis_at, blocks in shards:
        draws = jnp.exp(jax.random.uniform(jax.random.fold_in(own, axis_at), (blocks,), jnp.float32, low / len(shards), high / len(shards)))
        level = level * jnp.repeat(draws, shape[axis_at] // blocks).reshape([-1 if axis == axis_at else 1 for axis in range(len(shape))])
    return level


def normal_values(key, shape, width, most, pieces=(), kind=jnp.bfloat16):
    entries = width * jax.random.normal(key, shape, jnp.float32)
    if pieces:
        entries = entries * level_of(key, shape, pieces, -0.22, 0.18)
    return jnp.clip(entries, -most, most).astype(kind)


def setup_inputs(seed: int = 0, part: int = 0) -> dict:
    arg_keys = jax.random.split(jax.random.key(seed), 7)
    part_splits = jax.random.split(jax.random.fold_in(arg_keys[6], part), 7)
    return {
        "echo": normal_values(part_splits[0], (2, P_SIZE, R), 1.0, 6.0, ((1, 8), (2, 2))),
        "steer": normal_values(part_splits[1], (2, A, P_SIZE), (2 * P_SIZE) ** -0.5, 0.046875, ((1, 2), (2, 8))),
        "offsets": place_ends(jax.random.randint(part_splits[2], (NBLK,), 0, MAXOFF), jax.random.fold_in(part_splits[2], 1), 0, MAXOFF - 1).astype(jnp.int32),
        "taps": jnp.clip(0.1 + 0.9 * jax.random.uniform(part_splits[3], (NBLK, NTAP), jnp.float32) ** level_of(part_splits[3], (NBLK, NTAP), ((0, 8),), -0.2, 0.2), 0.1, 1.0),
        "centers": place_ends(jax.random.randint(part_splits[4], (R,), 0, A), jax.random.fold_in(part_splits[4], 1), 0, A - 1).astype(jnp.int32),
        "halves": place_ends(jax.random.randint(part_splits[5], (R,), A // 64, A // 8 + 1), jax.random.fold_in(part_splits[5], 1), A // 64, (A // 8 + 1) - 1).astype(jnp.int32),
    }


epsilon = 1e-6


def shift_segment(segment, offset, weights, length):
    margin = MAXOFF + NTAP - 1
    first_col = (margin - offset - (NTAP - 1)).astype(jnp.int32)
    window = lax.dynamic_slice_in_dim(segment, first_col, length + NTAP - 1, axis=2)
    result = jnp.zeros(segment.shape[:2] + (length,), jnp.float32)
    for tap_index in range(NTAP):
        lead_cols = NTAP - 1 - tap_index
        result = result + weights[tap_index] * window[:, :, lead_cols:lead_cols + length]
    return result


def reference(echo, steer, offsets, taps, centers, halves):
    margin = MAXOFF + NTAP - 1
    padded = jnp.pad(echo.astype(jnp.float32), ((0, 0), (0, 0), (margin, 0)))
    blocks = padded.reshape(2, NBLK, PBLK, margin + R)
    shifted = jax.vmap(lambda segment, offset, weights: shift_segment(segment, offset, weights, R),
                       in_axes=(1, 0, 0), out_axes=1)(blocks, offsets, taps)
    interp = shifted.reshape(2, P_SIZE, R).astype(jnp.bfloat16)
    interp = lax.optimization_barrier(interp).astype(jnp.float32)
    weights_full = steer.astype(jnp.float32)
    highest = lax.Precision.HIGHEST
    image_real = jnp.dot(interp[0].T, weights_full[0].T, precision=highest) - jnp.dot(interp[1].T, weights_full[1].T, precision=highest)
    image_imag = jnp.dot(interp[0].T, weights_full[1].T, precision=highest) + jnp.dot(interp[1].T, weights_full[0].T, precision=highest)
    image = lax.complex(image_real, image_imag)
    spectrum = jnp.fft.fft(image, axis=1)
    cells = jnp.arange(A, dtype=jnp.int32)
    distance = (cells[None, :] - centers[:, None]) % A
    distance = jnp.minimum(distance, (A - distance) % A)
    inside = (distance <= halves[:, None]).astype(jnp.float32)
    windowed = jnp.fft.fft(image * inside, axis=1)
    angle = (2.0 * math.pi / A) * centers.astype(jnp.float32)
    turned = lax.complex(jnp.cos(angle), jnp.sin(angle))
    cross = jnp.conj(windowed) * jnp.roll(windowed, -1, axis=1) * turned[:, None]
    numer = jnp.sum(jnp.imag(cross), axis=0)
    denom = jnp.sum(jnp.real(windowed) ** 2 + jnp.imag(windowed) ** 2, axis=0)
    slope = numer / (denom + epsilon)
    phase_error = jnp.cumsum(slope) - slope - jnp.arange(A, dtype=jnp.float32) * (jnp.sum(slope) / A)
    rotation = lax.complex(jnp.cos(phase_error), -jnp.sin(phase_error))
    corrected = jnp.fft.ifft(spectrum * rotation[None, :], axis=1)
    focused = jnp.stack([jnp.real(corrected), jnp.imag(corrected)])
    return focused, phase_error
```

```python
import functools
import math

import jax
import jax.numpy as jnp
import numpy as np
from jax import lax
from jax.experimental import pallas as pl
from jax.experimental.pallas import tpu as pltpu
from jax.sharding import PartitionSpec as P

PBLK = 64
NTAP = 4
LANES = 128
CHUNKS = 4
EPSILON = 1e-06
BF16 = jnp.bfloat16
F32 = jnp.float32
SENT = jnp.float16


def two_terms(table):
    high = table.astype(np.float32).astype(jnp.bfloat16)
    low = (table - high.astype(np.float64)).astype(np.float32).astype(jnp.bfloat16)
    return high, low


def dft_tables(length, direction):
    rows = length // LANES

    def waves(count, other, modulus):
        grid = np.outer(np.arange(count), np.arange(other)) % modulus
        angle = direction * 2.0 * math.pi / modulus * grid
        return np.cos(angle), np.sin(angle)

    scale = 1.0 if direction < 0 else 1.0 / length
    cos, sin = waves(rows, rows, rows)
    high, low = two_terms(scale * np.block([[cos, -sin], [sin, cos]]))
    over_rows = np.concatenate([high, high, low], axis=1)
    cos, sin = waves(LANES, LANES, LANES)
    high, low = two_terms(np.block([[cos, sin], [-sin, cos]]))
    over_lanes = np.concatenate([high, high, low], axis=0)
    cos, sin = waves(rows, LANES, length)
    twist = np.stack([cos, sin]).astype(np.float32)
    return over_rows, over_lanes, twist


def sum_tables(length):
    rows = length // LANES
    below = np.tril(np.ones((rows, rows)), -1)
    before = np.triu(np.ones((LANES, LANES)), 1)
    across = np.concatenate([before, np.ones((LANES, LANES))], axis=1)
    return (
        np.concatenate([below] * 3, axis=1).astype(jnp.bfloat16),
        np.concatenate([across] * 3, axis=0).astype(jnp.bfloat16),
    )


def interp_kernel(starts_ref, offsets_ref, taps_ref, echo_ref, left_ref):
    step = pl.program_id(0)
    lines = echo_ref.shape[2]
    sets = starts_ref.shape[0]
    size = lines // sets
    column = lax.broadcasted_iota(jnp.int32, (PBLK, lines), 1)
    sides = []
    for part in range(2):
        pieces = []
        for sub in range(LANES // PBLK):
            block = step * (LANES // PBLK) + sub
            offset = offsets_ref[block]
            value = echo_ref[part, sub * PBLK : (sub + 1) * PBLK, :].astype(F32)
            moved = pltpu.roll(value, offset, 1)
            moved = jnp.where(column >= offset, moved, 0.0)
            total = taps_ref[block * NTAP] * moved
            for tap in range(1, NTAP):
                moved = jnp.where(column >= 1, pltpu.roll(moved, 1, 1), 0.0)
                total = total + taps_ref[block * NTAP + tap] * moved
            pieces.append(total)
        both = jnp.concatenate(pieces, axis=0).astype(BF16).astype(F32)
        sides.append(jnp.transpose(both))
    real, imag = (side.astype(BF16) for side in sides)
    minus = (-sides[1]).astype(BF16)
    for at in range(sets):
        rows = slice(at * size, (at + 1) * size)
        first = pl.multiple_of(starts_ref[at], size)
        left_ref[0, pl.ds(first, size), :] = real[rows]
        left_ref[1, pl.ds(first, size), :] = minus[rows]
        first = pl.multiple_of(first + size, size)
        left_ref[0, pl.ds(first, size), :] = imag[rows]
        left_ref[1, pl.ds(first, size), :] = real[rows]


def interpolate(starts, offsets, taps, echo):
    pings, lines = echo.shape[1:]
    scalars = pl.BlockSpec(memory_space=pltpu.SMEM)
    return pl.pallas_call(
        interp_kernel,
        grid=(pings // LANES,),
        out_shape=jax.ShapeDtypeStruct((2, 2 * lines, pings), BF16),
        in_specs=[
            scalars,
            scalars,
            scalars,
            pl.BlockSpec((2, LANES, lines), lambda i: (0, i, 0)),
        ],
        out_specs=pl.BlockSpec((2, 2 * lines, LANES), lambda i: (0, 0, i)),
        compiler_params=pltpu.CompilerParams(vmem_limit_bytes=48 * 2**20),
        cost_estimate=pl.CostEstimate(flops=16 * pings * lines, bytes_accessed=12 * pings * lines, transcendentals=0),
        name="interp",
    )(starts, offsets, taps.reshape(-1), echo)


def image_kernel(left_ref, steer_ref, mine_ref, theirs_ref):
    contract = (((1,), (1,)), ((), ()))
    half = mine_ref.shape[0]
    for rows, out_ref in ((slice(half, None), theirs_ref), (slice(0, half), mine_ref)):
        total = lax.dot_general(left_ref[0, rows, :], steer_ref[0], contract, preferred_element_type=F32)
        total = total + lax.dot_general(left_ref[1, rows, :], steer_ref[1], contract, preferred_element_type=F32)
        out_ref[...] = total


def partial_image(left, steer, chunk):
    _, rows, pings = left.shape
    cells = steer.shape[1] // CHUNKS
    tile = math.gcd(cells, 512 if rows <= 512 else 128)
    steps = cells // tile
    half = rows // 2
    return pl.pallas_call(
        image_kernel,
        grid=(steps,),
        out_shape=(jax.ShapeDtypeStruct((half, cells), F32),) * 2,
        in_specs=[
            pl.BlockSpec((2, rows, pings), lambda i: (0, 0, 0)),
            pl.BlockSpec((2, tile, pings), lambda i: (0, chunk * steps + i, 0)),
        ],
        out_specs=(pl.BlockSpec((half, tile), lambda i: (0, i)),) * 2,
        compiler_params=pltpu.CompilerParams(vmem_limit_bytes=56 * 2**20),
        cost_estimate=pl.CostEstimate(
            flops=4 * rows * cells * pings, bytes_accessed=4 * cells * pings + 8 * half * cells, transcendentals=0
        ),
        name="image",
    )(left, steer)


def split_terms(value):
    high = value.astype(BF16)
    low = (value - high.astype(F32)).astype(BF16)
    return high, low


def forward(lines_pair, over_rows_ref, over_lanes_ref, twist_ref):
    rows = lines_pair[0][0].shape[0]
    grid = jnp.concatenate([jnp.concatenate(line, axis=0) for line in lines_pair], axis=1)
    high, low = split_terms(grid)
    first = jnp.dot(
        over_rows_ref[...], jnp.concatenate([high, low, high], axis=0), preferred_element_type=F32
    )
    twisted = []
    for at in range(len(lines_pair)):
        real = first[:rows, at * LANES : (at + 1) * LANES]
        imag = first[rows:, at * LANES : (at + 1) * LANES]
        cos, sin = twist_ref[0], twist_ref[1]
        twisted.append(jnp.concatenate([real * cos - imag * sin, real * sin + imag * cos], axis=1))
    high, low = split_terms(jnp.concatenate(twisted, axis=0))
    second = jnp.dot(
        jnp.concatenate([high, low, high], axis=1), over_lanes_ref[...], preferred_element_type=F32
    )
    return [second[at * rows : (at + 1) * rows] for at in range(len(lines_pair))]


def gradient_kernel(
    count,
    tile_ref,
    centers_ref,
    halves_ref,
    turn_ref,
    over_rows_ref,
    over_lanes_ref,
    twist_ref,
    *refs,
):
    own_refs, far_refs, (grid_ref, sums_ref) = refs[:CHUNKS], refs[CHUNKS:-2], refs[-2:]
    lines = own_refs[0].shape[0] // 2
    chunk_rows = own_refs[0].shape[1] // LANES
    rows = grid_ref.shape[1] // lines
    length = rows * LANES
    for chunk in range(CHUNKS):
        for piece in range(count):
            source = own_refs[chunk] if piece == 0 else far_refs[chunk].at[piece - 1]
            base = (tile_ref[piece] * CHUNKS + chunk) * chunk_rows
            for row in range(chunk_rows):
                first = pl.multiple_of((base + row) * lines, lines)
                for part in range(2):
                    grid_ref[part, pl.ds(first, lines), :] = source[
                        part * lines : (part + 1) * lines, row * LANES : (row + 1) * LANES
                    ]
    cell = lax.broadcasted_iota(jnp.int32, (rows, LANES), 0) * LANES + lax.broadcasted_iota(
        jnp.int32, (rows, LANES), 1
    )
    bottom = lax.broadcasted_iota(jnp.int32, (rows, LANES), 0) == rows - 1
    numer = jnp.zeros((rows, LANES), F32)
    denom = jnp.zeros((rows, LANES), F32)
    for pair in range(0, lines, 2):
        windowed = []
        for line in (pair, pair + 1):
            away = cell - centers_ref[line]
            away = jnp.where(away < 0, away + length, away)
            inside = jnp.minimum(away, length - away) <= halves_ref[line]
            windowed.append(
                [jnp.where(inside, grid_ref[part, pl.ds(line, rows, stride=lines), :], 0.0) for part in range(2)]
            )
        bins = forward(windowed, over_rows_ref, over_lanes_ref, twist_ref)
        for line, value in zip((pair, pair + 1), bins):
            real, imag = value[:, :LANES], value[:, LANES:]
            turned = []
            for side in (real, imag):
                up = pltpu.roll(side, rows - 1, 0)
                turned.append(jnp.where(bottom, pltpu.roll(up, LANES - 1, 1), up))
            next_real, next_imag = turned
            cross_real = real * next_real + imag * next_imag
            cross_imag = real * next_imag - imag * next_real
            numer = numer + (cross_real * turn_ref[1, line] + cross_imag * turn_ref[0, line])
            denom = denom + (real * real + imag * imag)
    sums_ref[0] = numer
    sums_ref[1] = denom


def gradient(tiles, centers, halves, turn, tables, own, far):
    count = tiles.shape[0]
    lines, cells = own[0].shape[0] // 2, own[0].shape[1]
    length = count * cells * CHUNKS
    scalars = pl.BlockSpec(memory_space=pltpu.SMEM)
    whole = pl.BlockSpec(memory_space=pltpu.VMEM)
    return pl.pallas_call(
        functools.partial(gradient_kernel, count),
        out_shape=(
            jax.ShapeDtypeStruct((2, length // LANES * lines, LANES), F32),
            jax.ShapeDtypeStruct((2, length // LANES, LANES), F32),
        ),
        in_specs=[scalars] * 4 + [whole] * (3 + 2 * CHUNKS),
        out_specs=(whole, whole),
        compiler_params=pltpu.CompilerParams(vmem_limit_bytes=40 * 2**20),
        cost_estimate=pl.CostEstimate(flops=2400 * lines * length, bytes_accessed=16 * lines * length, transcendentals=0),
        name="gradient",
    )(tiles, centers, halves, turn, *tables, *own, *far)


def spectrum_kernel(lines, over_rows_ref, over_lanes_ref, twist_ref, grid_ref, bins_ref):
    rows = grid_ref.shape[1] // lines
    for pair in range(0, lines, 2):
        both = [
            [grid_ref[part, pl.ds(line, rows, stride=lines), :] for part in range(2)] for line in (pair, pair + 1)
        ]
        for line, value in zip((pair, pair + 1), forward(both, over_rows_ref, over_lanes_ref, twist_ref)):
            bins_ref[line * rows : (line + 1) * rows, :] = value


def spectrum(tables, grid, lines):
    whole = pl.BlockSpec(memory_space=pltpu.VMEM)
    rows = grid.shape[1] // lines
    return pl.pallas_call(
        functools.partial(spectrum_kernel, lines),
        out_shape=jax.ShapeDtypeStruct((lines * rows, 2 * LANES), F32),
        in_specs=[whole] * 4,
        out_specs=whole,
        compiler_params=pltpu.CompilerParams(vmem_limit_bytes=40 * 2**20),
        cost_estimate=pl.CostEstimate(
            flops=2400 * lines * rows * LANES, bytes_accessed=16 * lines * rows * LANES, transcendentals=0
        ),
        name="spectrum",
    )(*tables, grid)


def three_terms(value):
    high, rest = value.astype(BF16), value
    rest = value - high.astype(F32)
    middle = rest.astype(BF16)
    low = (rest - middle.astype(F32)).astype(BF16)
    return [high, middle, low]


def focus_kernel(
    over_rows_ref, over_lanes_ref, twist_ref, below_ref, across_ref, sums_ref, bins_ref, out_ref, phase_ref, grid_ref
):
    rows = twist_ref.shape[1]
    lines = out_ref.shape[1]
    length = rows * LANES
    slope = sums_ref[0] / (sums_ref[1] + EPSILON)
    inner = jnp.dot(below_ref[...], jnp.concatenate(three_terms(slope), axis=0), preferred_element_type=F32)
    column = inner[rows - 8 :] + slope[rows - 8 :]
    outer = jnp.dot(jnp.concatenate(three_terms(column), axis=1), across_ref[...], preferred_element_type=F32)
    prefix = inner + outer[7:8, :LANES]
    place = lax.broadcasted_iota(jnp.int32, (rows, LANES), 0) + rows * lax.broadcasted_iota(
        jnp.int32, (rows, LANES), 1
    )
    phase = prefix - place.astype(F32) * (outer[7:8, LANES:] * (1.0 / length))
    phase_ref[...] = phase
    cos, sin = jnp.cos(phase), jnp.sin(phase)
    for pair in range(0, lines, 2):
        fixed = []
        for line in (pair, pair + 1):
            real = bins_ref[line * rows : (line + 1) * rows, :LANES]
            imag = bins_ref[line * rows : (line + 1) * rows, LANES:]
            fixed.append(jnp.concatenate([real * cos + imag * sin, imag * cos - real * sin], axis=1))
        high, low = split_terms(jnp.concatenate(fixed, axis=0))
        first = jnp.dot(
            jnp.concatenate([high, low, high], axis=1), over_lanes_ref[...], preferred_element_type=F32
        )
        twisted = []
        for at in range(2):
            real = first[at * rows : (at + 1) * rows, :LANES]
            imag = first[at * rows : (at + 1) * rows, LANES:]
            turn_cos, turn_sin = twist_ref[0], twist_ref[1]
            twisted.append(
                jnp.concatenate([real * turn_cos - imag * turn_sin, real * turn_sin + imag * turn_cos], axis=0)
            )
        high, low = split_terms(jnp.concatenate(twisted, axis=1))
        second = jnp.dot(
            over_rows_ref[...], jnp.concatenate([high, low, high], axis=0), preferred_element_type=F32
        )
        for at in range(2):
            for part in range(2):
                grid_ref[part, pl.ds(pair + at, rows, stride=lines), :] = second[
                    part * rows : (part + 1) * rows, at * LANES : (at + 1) * LANES
                ]
    for row in range(rows):
        for part in range(2):
            out_ref[part, :, row * LANES : (row + 1) * LANES] = grid_ref[part, row * lines : (row + 1) * lines, :]


def focus(tables, prefix_tables, sums, bins, lines):
    whole = pl.BlockSpec(memory_space=pltpu.VMEM)
    rows = sums.shape[1]
    return pl.pallas_call(
        focus_kernel,
        out_shape=(
            jax.ShapeDtypeStruct((2, lines, rows * LANES), F32),
            jax.ShapeDtypeStruct((rows, LANES), F32),
        ),
        in_specs=[whole] * 7,
        out_specs=(whole, whole),
        scratch_shapes=[pltpu.VMEM((2, rows * lines, LANES), F32)],
        compiler_params=pltpu.CompilerParams(vmem_limit_bytes=40 * 2**20),
        cost_estimate=pl.CostEstimate(
            flops=2400 * lines * rows * LANES, bytes_accessed=16 * lines * rows * LANES, transcendentals=0
        ),
        name="focus",
    )(*tables, *prefix_tables, sums, bins)


def swap(value, axis, bit):
    count = lax.axis_size(axis)
    return lax.ppermute(value, axis, [(at, at ^ bit) for at in range(count)])


def total_over(value, axis):
    count = lax.axis_size(axis)
    bit = 1
    while bit < count:
        value = value + swap(value, axis, bit)
        bit *= 2
    return value


def gather_lines(value, axis):
    if lax.axis_size(axis) != 2:
        return lax.all_gather(value, axis, axis=2, tiled=True)
    other = swap(value, axis, 1)
    first = lax.axis_index(axis) == 0
    return jnp.concatenate([jnp.where(first, value, other), jnp.where(first, other, value)], axis=2)


def largest(value):
    return jnp.max(jnp.abs(value)).astype(F32)


def common_scale(echo, taps, steer):
    local = jnp.stack([largest(echo), largest(taps), largest(steer)])
    local = jnp.broadcast_to(local[:, None, None], (3, 8, LANES))
    for axis in ("ping", "rng"):
        local = functools.reduce(jnp.maximum, [local] + [swap(local, axis, at) for at in range(1, lax.axis_size(axis))])
    most = local[:, 0, 0]
    terms = 2 * NTAP * steer.shape[2] * lax.axis_size("ping")
    bound = jnp.clip(terms * most[0] * most[1] * most[2], 1e-30, 1e30)
    power = jnp.clip(jnp.floor(jnp.log2(2.0**15 / bound)), -100.0, 100.0)
    return jnp.exp2(power), jnp.exp2(-power)


def start_rows(pings, tiles, lines):
    me, tile = lax.axis_index("ping"), lax.axis_index("rng")
    owner = jnp.arange(pings * tiles, dtype=jnp.int32)
    apart = (owner // tiles) ^ me
    slot = jnp.zeros_like(apart)
    bit = 1
    while bit < pings:
        slot = 2 * slot + (apart & bit) // bit
        bit *= 2
    return (slot * tiles + (owner % tiles - tile) % tiles) * (2 * lines)


def scatter_sum(mine, theirs, scale):
    up, down = scale
    count = lax.axis_size("ping")
    value = mine + swap(theirs, "ping", 1)
    bit = 2
    while bit < count:
        half = value.shape[0] // 2
        got = swap((value[half:] * up).astype(SENT), "ping", bit)
        value = value[:half] + got.astype(F32) * down
        bit *= 2
    return value


def on_device(echo, steer, offsets, taps, centers, halves):
    pings = lax.axis_size("ping")
    tiles = lax.axis_size("rng")
    tile = lax.axis_index("rng")
    lines = centers.shape[0]
    length = steer.shape[1] * tiles

    echo_lines = gather_lines(echo, "rng")
    scale = common_scale(echo, taps, steer)
    left = interpolate(start_rows(pings, tiles, lines), offsets, taps, echo_lines)
    own, far = [], []
    for chunk in range(CHUNKS):
        total = scatter_sum(*partial_image(left, steer, chunk), scale)
        own.append(total[: 2 * lines])
        pieces = []
        for step in range(1, tiles):
            send = (total[2 * lines * step : 2 * lines * (step + 1)] * scale[0]).astype(SENT)
            got = lax.ppermute(send, "rng", [(at, (at + step) % tiles) for at in range(tiles)])
            pieces.append(got.astype(F32) * scale[1])
        far.append(jnp.stack(pieces))

    angle = 2.0 * math.pi / length * centers.astype(F32)
    turn = jnp.stack([jnp.cos(angle), jnp.sin(angle)])
    owners = (tile - jnp.arange(tiles, dtype=jnp.int32)) % tiles
    tables = [jnp.asarray(table) for table in dft_tables(length, -1.0)]
    grid, sums = gradient(owners, centers, halves, turn, tables, own, far)
    sums = total_over(total_over(sums, "ping"), "rng")
    bins = spectrum(tables, grid, lines)
    tables = [jnp.asarray(table) for table in dft_tables(length, 1.0)]
    prefix_tables = [jnp.asarray(table) for table in sum_tables(length)]
    focused, phase = focus(tables, prefix_tables, sums, bins, lines)
    return (focused, phase.T.reshape(-1))


def solution(mesh):
    in_specs = (
        P(None, ("leg", "ping"), "rng"),
        P(None, ("leg", "rng"), "ping"),
        P(("leg", "ping")),
        P(("leg", "ping"), None),
        P(("leg", "ping", "rng")),
        P(("leg", "ping", "rng")),
    )
    out_specs = (P(None, ("leg", "ping", "rng"), None), P("leg"))
    return jax.shard_map(
        on_device, mesh=mesh, in_specs=in_specs, out_specs=out_specs, check_vma=False
    )
```

```python
import functools
import math

import jax
import jax.numpy as jnp
import numpy as np
from jax import lax
from jax.experimental import pallas as pl
from jax.experimental.pallas import tpu as pltpu
from jax.sharding import PartitionSpec as P

PBLK = 64
NTAP = 4
MARGIN = 24
LANES = 128
SHARES = (12, 12, 8)
EPSILON = 1e-06
BF16 = jnp.bfloat16
F32 = jnp.float32
SENT = jnp.float16


def cuts_of(cells):
    units, total = cells // LANES, sum(SHARES)
    sizes = [units * share // total for share in SHARES]
    if units % total:
        count = math.gcd(units, len(SHARES))
        sizes = [units // count] * count
    cuts, first = [], 0
    for size in sizes:
        cuts.append((first * LANES, size * LANES))
        first += size
    return cuts


def two_terms(table):
    high = table.astype(np.float32).astype(jnp.bfloat16)
    low = (table - high.astype(np.float64)).astype(np.float32).astype(jnp.bfloat16)
    return high, low


def dft_tables(length, direction):
    rows = length // LANES

    def waves(count, other, modulus):
        grid = np.outer(np.arange(count), np.arange(other)) % modulus
        angle = direction * 2.0 * math.pi / modulus * grid
        return np.cos(angle), np.sin(angle)

    scale = 1.0 if direction < 0 else 1.0 / length
    cos, sin = waves(rows, rows, rows)
    high, low = two_terms(scale * np.block([[cos, -sin], [sin, cos]]))
    over_rows = np.concatenate([high, high, low], axis=1)
    cos, sin = waves(LANES, LANES, LANES)
    high, low = two_terms(np.block([[cos, sin], [-sin, cos]]))
    over_lanes = np.concatenate([high, high, low], axis=0)
    cos, sin = waves(rows, LANES, length)
    twist = np.stack([cos, sin]).astype(np.float32)
    return over_rows, over_lanes, twist


def sum_tables(length):
    rows = length // LANES
    below = np.tril(np.ones((rows, rows)), -1)
    before = np.triu(np.ones((LANES, LANES)), 1)
    across = np.concatenate([before, np.ones((LANES, LANES))], axis=1)
    return (
        np.concatenate([below] * 3, axis=1).astype(jnp.bfloat16),
        np.concatenate([across] * 3, axis=0).astype(jnp.bfloat16),
    )


def interp_kernel(starts_ref, offsets_ref, taps_ref, echo_ref, left_ref, turned_ref):
    step = pl.program_id(0)
    lines = echo_ref.shape[2]
    sets = starts_ref.shape[0]
    size = lines // sets
    blocks = LANES // PBLK
    lane = lax.broadcasted_iota(jnp.int32, (size, LANES), 1)
    weights, rows_back = [], []
    for sub in range(blocks):
        block = step * blocks + sub
        here = lane // PBLK == sub
        weights.append([jnp.where(here, taps_ref[tap, block], 0.0) for tap in range(NTAP)])
        rows_back.append(MARGIN - offsets_ref[block])

    for part in range(2):
        turned_ref[part, :MARGIN, :] = jnp.zeros((MARGIN, LANES), F32)
        turned_ref[part, MARGIN:, :] = jnp.transpose(echo_ref[part].astype(F32))

    def line_set(at, first):
        sides = []
        for part in range(2):
            total = None
            for tap in range(NTAP):
                for sub in range(blocks):
                    rows = turned_ref[part, pl.ds(rows_back[sub] + (at * size - tap), size), :]
                    term = weights[sub][tap] * rows
                    total = term if total is None else total + term
            sides.append(total)
        real, imag = sides
        left_ref[0, pl.ds(first, size), :] = real.astype(BF16)
        left_ref[1, pl.ds(first, size), :] = (-imag).astype(BF16)
        left_ref[0, pl.ds(first + size, size), :] = imag.astype(BF16)
        left_ref[1, pl.ds(first + size, size), :] = real.astype(BF16)

    for at in range(sets):
        line_set(at, pl.multiple_of(starts_ref[at], size))


def interpolate(starts, offsets, taps, echo):
    pings, lines = echo.shape[1:]
    scalars = pl.BlockSpec(memory_space=pltpu.SMEM)
    return pl.pallas_call(
        interp_kernel,
        grid=(pings // LANES,),
        out_shape=jax.ShapeDtypeStruct((2, 2 * lines, pings), BF16),
        in_specs=[
            scalars,
            scalars,
            scalars,
            pl.BlockSpec((2, LANES, lines), lambda i: (0, i, 0)),
        ],
        out_specs=pl.BlockSpec((2, 2 * lines, LANES), lambda i: (0, 0, i)),
        scratch_shapes=[pltpu.VMEM((2, MARGIN + lines, LANES), F32)],
        compiler_params=pltpu.CompilerParams(vmem_limit_bytes=48 * 2**20),
        cost_estimate=pl.CostEstimate(flops=16 * pings * lines, bytes_accessed=12 * pings * lines, transcendentals=0),
        name="interp",
    )(starts, offsets, taps, echo)


def largest_kernel(echo_ref, taps_ref, steer_ref, most_ref, here_ref, sems):
    pieces, sets, rows, width = here_ref.shape
    copies = [
        pltpu.make_async_copy(steer_ref.at[:, pl.ds(at * rows, rows), :], here_ref.at[at], sems.at[at])
        for at in range(pieces)
    ]
    for copy in copies:
        copy.start()
    for at, ref in enumerate((echo_ref, taps_ref)):
        most_ref[at] = jnp.full(most_ref.shape[1:], jnp.max(jnp.abs(ref[...]).astype(F32)), F32)
    most = jnp.zeros((16, width), here_ref.dtype)
    for at, copy in enumerate(copies):
        copy.wait()
        most = jnp.maximum(most, jnp.max(jnp.abs(here_ref[at]).reshape(sets * rows // 16, 16, width), axis=0))
    most_ref[2] = jnp.full(most_ref.shape[1:], jnp.max(most.astype(F32)), F32)


def largest(echo, taps, steer):
    sets, rows, width = steer.shape
    pieces = max(1, rows // 512)
    whole = pl.BlockSpec(memory_space=pltpu.VMEM)
    return pl.pallas_call(
        largest_kernel,
        out_shape=jax.ShapeDtypeStruct((3, 8, LANES), F32),
        in_specs=[whole, whole, pl.BlockSpec(memory_space=pl.ANY)],
        out_specs=whole,
        scratch_shapes=[
            pltpu.VMEM((pieces, sets, rows // pieces, width), steer.dtype),
            pltpu.SemaphoreType.DMA((pieces,)),
        ],
        compiler_params=pltpu.CompilerParams(vmem_limit_bytes=56 * 2**20),
        cost_estimate=pl.CostEstimate(flops=steer.size, bytes_accessed=2 * steer.size, transcendentals=0),
        name="largest",
    )(echo, taps, steer)


def image_kernel(left_ref, steer_ref, mine_ref, theirs_ref):
    contract = (((1,), (1,)), ((), ()))
    half = mine_ref.shape[0]
    for rows, out_ref in ((slice(half, None), theirs_ref), (slice(0, half), mine_ref)):
        total = lax.dot_general(left_ref[0, rows, :], steer_ref[0], contract, preferred_element_type=F32)
        total = total + lax.dot_general(left_ref[1, rows, :], steer_ref[1], contract, preferred_element_type=F32)
        out_ref[...] = total


def partial_image(left, steer, first, cells):
    _, rows, pings = left.shape
    tile = math.gcd(math.gcd(first, cells), 512 if rows <= 512 else 128)
    half = rows // 2
    return pl.pallas_call(
        image_kernel,
        grid=(cells // tile,),
        out_shape=(jax.ShapeDtypeStruct((half, cells), F32),) * 2,
        in_specs=[
            pl.BlockSpec(memory_space=pltpu.VMEM),
            pl.BlockSpec((2, tile, pings), lambda i: (0, first // tile + i, 0)),
        ],
        out_specs=(pl.BlockSpec((half, tile), lambda i: (0, i)),) * 2,
        compiler_params=pltpu.CompilerParams(vmem_limit_bytes=40 * 2**20),
        cost_estimate=pl.CostEstimate(flops=cells, bytes_accessed=cells, transcendentals=0),
        name="image",
    )(left, steer)


def split_terms(value):
    high = value.astype(BF16)
    low = (value - high.astype(F32)).astype(BF16)
    return high, low


def forward(lines_pair, over_rows_ref, over_lanes_ref, twist_ref):
    rows = lines_pair[0][0].shape[0]
    grid = jnp.concatenate([jnp.concatenate(line, axis=0) for line in lines_pair], axis=1)
    high, low = split_terms(grid)
    first = jnp.dot(
        over_rows_ref[...], jnp.concatenate([high, low, high], axis=0), preferred_element_type=F32
    )
    twisted = []
    for at in range(len(lines_pair)):
        real = first[:rows, at * LANES : (at + 1) * LANES]
        imag = first[rows:, at * LANES : (at + 1) * LANES]
        cos, sin = twist_ref[0], twist_ref[1]
        twisted.append(jnp.concatenate([real * cos - imag * sin, real * sin + imag * cos], axis=1))
    high, low = split_terms(jnp.concatenate(twisted, axis=0))
    second = jnp.dot(
        jnp.concatenate([high, low, high], axis=1), over_lanes_ref[...], preferred_element_type=F32
    )
    return [second[at * rows : (at + 1) * rows] for at in range(len(lines_pair))]


def gradient_kernel(
    count,
    cuts,
    tile_ref,
    centers_ref,
    halves_ref,
    turn_ref,
    down_ref,
    over_rows_ref,
    over_lanes_ref,
    twist_ref,
    *refs,
):
    own_refs, far_refs, (grid_ref, sums_ref) = refs[: len(cuts)], refs[len(cuts) : -2], refs[-2:]
    lines = own_refs[0].shape[0] // 2
    rows = grid_ref.shape[1] // lines
    length = rows * LANES
    down = jnp.concatenate([down_ref[...]] * (lines // 8), axis=0)
    for (start, cells), own_ref, far_ref in zip(cuts, own_refs, far_refs):
        for piece in range(count):
            source = own_ref if piece == 0 else far_ref.at[piece - 1]
            base = tile_ref[piece] * (rows // count) + start // LANES
            for row in range(cells // LANES):
                first = pl.multiple_of((base + row) * lines, lines)
                for part in range(2):
                    value = source[part * lines : (part + 1) * lines, row * LANES : (row + 1) * LANES]
                    grid_ref[part, pl.ds(first, lines), :] = value * down
    cell = lax.broadcasted_iota(jnp.int32, (rows, LANES), 0) * LANES + lax.broadcasted_iota(
        jnp.int32, (rows, LANES), 1
    )
    bottom = lax.broadcasted_iota(jnp.int32, (rows, LANES), 0) == rows - 1
    numer = jnp.zeros((rows, LANES), F32)
    denom = jnp.zeros((rows, LANES), F32)
    for pair in range(0, lines, 2):
        windowed = []
        for line in (pair, pair + 1):
            away = cell - centers_ref[line]
            away = jnp.where(away < 0, away + length, away)
            inside = jnp.minimum(away, length - away) <= halves_ref[line]
            windowed.append(
                [jnp.where(inside, grid_ref[part, pl.ds(line, rows, stride=lines), :], 0.0) for part in range(2)]
            )
        bins = forward(windowed, over_rows_ref, over_lanes_ref, twist_ref)
        for line, value in zip((pair, pair + 1), bins):
            real, imag = value[:, :LANES], value[:, LANES:]
            turned = []
            for side in (real, imag):
                up = pltpu.roll(side, rows - 1, 0)
                turned.append(jnp.where(bottom, pltpu.roll(up, LANES - 1, 1), up))
            next_real, next_imag = turned
            cross_real = real * next_real + imag * next_imag
            cross_imag = real * next_imag - imag * next_real
            numer = numer + (cross_real * turn_ref[1, line] + cross_imag * turn_ref[0, line])
            denom = denom + (real * real + imag * imag)
    sums_ref[0] = numer
    sums_ref[1] = denom


def gradient(tiles, cuts, centers, halves, turn, down, tables, own, far):
    count = tiles.shape[0]
    lines = own[0].shape[0] // 2
    length = count * sum(cells for _, cells in cuts)
    scalars = pl.BlockSpec(memory_space=pltpu.SMEM)
    whole = pl.BlockSpec(memory_space=pltpu.VMEM)
    return pl.pallas_call(
        functools.partial(gradient_kernel, count, cuts),
        out_shape=(
            jax.ShapeDtypeStruct((2, length // LANES * lines, LANES), F32),
            jax.ShapeDtypeStruct((2, length // LANES, LANES), F32),
        ),
        in_specs=[scalars] * 4 + [whole] * (4 + 2 * len(cuts)),
        out_specs=(whole, whole),
        compiler_params=pltpu.CompilerParams(vmem_limit_bytes=40 * 2**20),
        cost_estimate=pl.CostEstimate(flops=2400 * lines * length, bytes_accessed=16 * lines * length, transcendentals=0),
        name="gradient",
    )(tiles, centers, halves, turn, down, *tables, *own, *far)


def spectrum_kernel(lines, over_rows_ref, over_lanes_ref, twist_ref, grid_ref, bins_ref):
    rows = grid_ref.shape[1] // lines
    for pair in range(0, lines, 2):
        both = [
            [grid_ref[part, pl.ds(line, rows, stride=lines), :] for part in range(2)] for line in (pair, pair + 1)
        ]
        for line, value in zip((pair, pair + 1), forward(both, over_rows_ref, over_lanes_ref, twist_ref)):
            bins_ref[line * rows : (line + 1) * rows, :] = value


def spectrum(tables, grid, lines):
    whole = pl.BlockSpec(memory_space=pltpu.VMEM)
    rows = grid.shape[1] // lines
    return pl.pallas_call(
        functools.partial(spectrum_kernel, lines),
        out_shape=jax.ShapeDtypeStruct((lines * rows, 2 * LANES), F32),
        in_specs=[whole] * 4,
        out_specs=whole,
        compiler_params=pltpu.CompilerParams(vmem_limit_bytes=40 * 2**20),
        cost_estimate=pl.CostEstimate(
            flops=2400 * lines * rows * LANES, bytes_accessed=16 * lines * rows * LANES, transcendentals=0
        ),
        name="spectrum",
    )(*tables, grid)


def three_terms(value):
    high, rest = value.astype(BF16), value
    rest = value - high.astype(F32)
    middle = rest.astype(BF16)
    low = (rest - middle.astype(F32)).astype(BF16)
    return [high, middle, low]


def focus_kernel(
    over_rows_ref, over_lanes_ref, twist_ref, below_ref, across_ref, sums_ref, bins_ref, out_ref, phase_ref, grid_ref, turned_ref
):
    rows = twist_ref.shape[1]
    lines = out_ref.shape[1]
    length = rows * LANES
    slope = sums_ref[0] / (sums_ref[1] + EPSILON)
    inner = jnp.dot(below_ref[...], jnp.concatenate(three_terms(slope), axis=0), preferred_element_type=F32)
    column = inner[rows - 8 :] + slope[rows - 8 :]
    outer = jnp.dot(jnp.concatenate(three_terms(column), axis=1), across_ref[...], preferred_element_type=F32)
    prefix = inner + outer[7:8, :LANES]
    place = lax.broadcasted_iota(jnp.int32, (rows, LANES), 0) + rows * lax.broadcasted_iota(
        jnp.int32, (rows, LANES), 1
    )
    phase = prefix - place.astype(F32) * (outer[7:8, LANES:] * (1.0 / length))
    turned_ref[...] = jnp.transpose(phase)
    runs = LANES // rows
    phase_ref[...] = jnp.concatenate(
        [turned_ref[pl.ds(at, rows, stride=runs), :] for at in range(runs)], axis=1
    )
    cos, sin = jnp.cos(phase), jnp.sin(phase)
    for pair in range(0, lines, 2):
        fixed = []
        for line in (pair, pair + 1):
            real = bins_ref[line * rows : (line + 1) * rows, :LANES]
            imag = bins_ref[line * rows : (line + 1) * rows, LANES:]
            fixed.append(jnp.concatenate([real * cos + imag * sin, imag * cos - real * sin], axis=1))
        high, low = split_terms(jnp.concatenate(fixed, axis=0))
        first = jnp.dot(
            jnp.concatenate([high, low, high], axis=1), over_lanes_ref[...], preferred_element_type=F32
        )
        twisted = []
        for at in range(2):
            real = first[at * rows : (at + 1) * rows, :LANES]
            imag = first[at * rows : (at + 1) * rows, LANES:]
            turn_cos, turn_sin = twist_ref[0], twist_ref[1]
            twisted.append(
                jnp.concatenate([real * turn_cos - imag * turn_sin, real * turn_sin + imag * turn_cos], axis=0)
            )
        high, low = split_terms(jnp.concatenate(twisted, axis=1))
        second = jnp.dot(
            over_rows_ref[...], jnp.concatenate([high, low, high], axis=0), preferred_element_type=F32
        )
        for at in range(2):
            for part in range(2):
                grid_ref[part, pl.ds(pair + at, rows, stride=lines), :] = second[
                    part * rows : (part + 1) * rows, at * LANES : (at + 1) * LANES
                ]
    for row in range(rows):
        for part in range(2):
            out_ref[part, :, row * LANES : (row + 1) * LANES] = grid_ref[part, row * lines : (row + 1) * lines, :]


def focus(tables, prefix_tables, sums, bins, lines):
    whole = pl.BlockSpec(memory_space=pltpu.VMEM)
    rows = sums.shape[1]
    return pl.pallas_call(
        focus_kernel,
        out_shape=(
            jax.ShapeDtypeStruct((2, lines, rows * LANES), F32),
            jax.ShapeDtypeStruct((rows, LANES), F32),
        ),
        in_specs=[whole] * 7,
        out_specs=(whole, whole),
        scratch_shapes=[pltpu.VMEM((2, rows * lines, LANES), F32), pltpu.VMEM((LANES, rows), F32)],
        compiler_params=pltpu.CompilerParams(vmem_limit_bytes=40 * 2**20),
        cost_estimate=pl.CostEstimate(
            flops=2400 * lines * rows * LANES, bytes_accessed=16 * lines * rows * LANES, transcendentals=0
        ),
        name="focus",
    )(*tables, *prefix_tables, sums, bins)


def swap(value, axis, bit):
    count = lax.axis_size(axis)
    return lax.ppermute(value, axis, [(at, at ^ bit) for at in range(count)])


def total_over(value, pairs):
    for at in range(0, len(pairs), 2):
        (axis, bit), *more = sorted(pairs[at : at + 2])
        first = swap(value, axis, bit)
        for other, other_bit in more:
            second = swap(value, other, other_bit)
            if other == axis:
                third = swap(value, axis, bit ^ other_bit)
            else:
                count, inner = lax.axis_size(axis), lax.axis_size(other)
                both = [(i, ((i // inner) ^ bit) * inner + ((i % inner) ^ other_bit)) for i in range(count * inner)]
                third = lax.ppermute(value, (axis, other), both)
            value, first = value + first, second + third
        value = value + first
    return value


def gather_lines(value, axis):
    if lax.axis_size(axis) != 2:
        return lax.all_gather(value, axis, axis=2, tiled=True)
    other = swap(value, axis, 1)
    first = lax.axis_index(axis) == 0
    return jnp.concatenate([jnp.where(first, value, other), jnp.where(first, other, value)], axis=2)


def scale_of(known, terms):
    bound = jnp.clip(terms * known[0] * known[1] * known[2], 1e-30, 1e30)
    power = jnp.clip(jnp.floor(jnp.log2(2.0**15 / bound)), -100.0, 100.0)
    return lax.optimization_barrier((jnp.exp2(power), jnp.exp2(-power)))


def start_rows(pings, tiles, lines):
    me, tile = lax.axis_index("ping"), lax.axis_index("rng")
    owner = jnp.arange(pings * tiles, dtype=jnp.int32)
    apart = (owner // tiles) ^ me
    slot = jnp.zeros_like(apart)
    bit = 1
    while bit < pings:
        slot = 2 * slot + (apart & bit) // bit
        bit *= 2
    return (slot * tiles + (owner % tiles - tile) % tiles) * (2 * lines)


def tie(value, *others):
    return lax.optimization_barrier((value, *others))[0]


def packed(value):
    return value[value.shape[0] // 2 :].astype(SENT)


def merged(value, got):
    return value[: value.shape[0] // 2] + got.astype(F32)


def on_device(echo, steer, offsets, taps, centers, halves):
    pings = lax.axis_size("ping")
    tiles = lax.axis_size("rng")
    tile = lax.axis_index("rng")
    lines = centers.shape[0]
    length = steer.shape[1] * tiles
    cuts = cuts_of(steer.shape[1])

    echo_lines = gather_lines(echo, "rng")
    taps = taps.T
    known = largest(echo, taps, steer)
    known = jnp.maximum(known, swap(known, "ping", 1))
    bits = [1 << at for at in range(1, pings.bit_length() - 1)]
    steps = [("ping", bit) for bit in bits] + [("rng", 1 << at) for at in range(tiles.bit_length() - 1)]
    echo_lines = tie(echo_lines, known)
    got = swap(known, *steps[0])
    left = interpolate(start_rows(pings, tiles, lines), offsets, taps, echo_lines)
    known = jnp.maximum(known, tie(got, left))

    count = len(cuts)
    totals, moving = [None] * count, [None] * count

    def advance(at, stage, gate):
        got = moving[at] if gate is None else tie(moving[at], gate)
        totals[at] = (totals[at] + got) * up[0, 0] if stage == 0 else merged(totals[at], got)
        if stage == len(bits):
            return totals[at]
        send = packed(totals[at])
        moving[at] = swap(send, "ping", bits[stage])
        return send

    gate = known
    for at in range(count + 1):
        if at < count:
            left = tie(left, gate)
            totals[at], theirs = partial_image(left, steer, *cuts[at])
            moving[at] = swap(theirs, "ping", 1)
            gate = theirs
        for step in steps[1:] if at == 1 else steps[1:2] if at == 0 else []:
            if at == 0 or step != steps[1]:
                known = jnp.maximum(known, tie(swap(known, *step), gate))
                gate = known
        if at == 1:
            up, down = scale_of(known, 2.0 * NTAP * steer.shape[2] * pings)
        for stage in range(min(at, 2)):
            gate = advance(at - 1 - stage, stage, gate)
    waiting = [(count - 1, 1)] + [(at, stage) for at in range(count) for stage in range(2, len(bits) + 1)]
    for at, stage in sorted(waiting, key=lambda item: (item[0] + 2 * item[1], item[1])):
        advance(at, stage, gate if stage == 1 else None)
    own, far = [], []
    for total in totals:
        own.append(total[: 2 * lines])
        pieces = []
        for step in range(1, tiles):
            send = total[2 * lines * step : 2 * lines * (step + 1)]
            pieces.append(lax.ppermute(send, "rng", [(at, (at + step) % tiles) for at in range(tiles)]))
        far.append(jnp.stack(pieces))

    angle = 2.0 * math.pi / length * centers.astype(F32)
    turn = jnp.stack([jnp.cos(angle), jnp.sin(angle)])
    owners = (tile - jnp.arange(tiles, dtype=jnp.int32)) % tiles
    tables = [jnp.asarray(table) for table in dft_tables(length, -1.0)]
    grid, sums = gradient(owners, cuts, centers, halves, turn, down, tables, own, far)
    pairs = [("ping", 1)] + [("rng", 1 << at) for at in range(tiles.bit_length() - 1)] + [("ping", bit) for bit in bits]
    sums = total_over(sums, pairs)
    bins = spectrum(tables, grid, lines)
    tables = [jnp.asarray(table) for table in dft_tables(length, 1.0)]
    prefix_tables = [jnp.asarray(table) for table in sum_tables(length)]
    focused, phase = focus(tables, prefix_tables, sums, bins, lines)
    return (focused, phase.reshape(-1))


def solution(mesh):
    in_specs = (
        P(None, ("leg", "ping"), "rng"),
        P(None, ("leg", "rng"), "ping"),
        P(("leg", "ping")),
        P(("leg", "ping"), None),
        P(("leg", "ping", "rng")),
        P(("leg", "ping", "rng")),
    )
    out_specs = (P(None, ("leg", "ping", "rng"), None), P("leg"))
    return jax.shard_map(
        on_device, mesh=mesh, in_specs=in_specs, out_specs=out_specs, check_vma=False
    )
```

```python
import functools
import math

import jax
import jax.numpy as jnp
import numpy as np
from jax import lax
from jax.experimental import pallas as pl
from jax.experimental.pallas import tpu as pltpu
from jax.sharding import PartitionSpec as P

PBLK = 64
NTAP = 4
MARGIN = 24
LANES = 128
SHARES = (8, 8, 8, 4, 4)
STAGES = (0, 1, 2)
EPSILON = 1e-06
BF16 = jnp.bfloat16
F32 = jnp.float32
SENT = jnp.float16


def cuts_of(cells):
    units, total = cells // LANES, sum(SHARES)
    sizes = [units * share // total for share in SHARES]
    if units % total:
        count = math.gcd(units, len(SHARES))
        sizes = [units // count] * count
    cuts, first = [], 0
    for size in sizes:
        cuts.append((first * LANES, size * LANES))
        first += size
    return cuts


def two_terms(table):
    high = table.astype(np.float32).astype(jnp.bfloat16)
    low = (table - high.astype(np.float64)).astype(np.float32).astype(jnp.bfloat16)
    return high, low


def dft_tables(length, direction):
    rows = length // LANES

    def waves(count, other, modulus):
        grid = np.outer(np.arange(count), np.arange(other)) % modulus
        angle = direction * 2.0 * math.pi / modulus * grid
        return np.cos(angle), np.sin(angle)

    scale = 1.0 if direction < 0 else 1.0 / length
    cos, sin = waves(rows, rows, rows)
    high, low = two_terms(scale * np.block([[cos, -sin], [sin, cos]]))
    over_rows = np.concatenate([high, high, low], axis=1)
    cos, sin = waves(LANES, LANES, LANES)
    high, low = two_terms(np.block([[cos, sin], [-sin, cos]]))
    over_lanes = np.concatenate([high, high, low], axis=0)
    cos, sin = waves(rows, LANES, length)
    twist = np.stack([cos, sin]).astype(np.float32)
    return over_rows, over_lanes, twist


def sum_tables(length):
    rows = length // LANES
    below = np.tril(np.ones((rows, rows)), -1)
    before = np.triu(np.ones((LANES, LANES)), 1)
    across = np.concatenate([before, np.ones((LANES, LANES))], axis=1)
    return (
        np.concatenate([below] * 3, axis=1).astype(jnp.bfloat16),
        np.concatenate([across] * 3, axis=0).astype(jnp.bfloat16),
    )


def interp_kernel(starts_ref, offsets_ref, taps_ref, echo_ref, left_ref, turned_ref):
    step = pl.program_id(0)
    lines = echo_ref.shape[2]
    sets = starts_ref.shape[0]
    size = lines // sets
    blocks = LANES // PBLK
    lane = lax.broadcasted_iota(jnp.int32, (size, LANES), 1)
    weights, rows_back = [], []
    for sub in range(blocks):
        block = step * blocks + sub
        here = lane // PBLK == sub
        weights.append([jnp.where(here, taps_ref[tap, block], 0.0) for tap in range(NTAP)])
        rows_back.append(MARGIN - offsets_ref[block])

    for part in range(2):
        turned_ref[part, :MARGIN, :] = jnp.zeros((MARGIN, LANES), F32)
        turned_ref[part, MARGIN:, :] = jnp.transpose(echo_ref[part].astype(F32))

    def line_set(at, first):
        sides = []
        for part in range(2):
            total = None
            for tap in range(NTAP):
                for sub in range(blocks):
                    rows = turned_ref[part, pl.ds(rows_back[sub] + (at * size - tap), size), :]
                    term = weights[sub][tap] * rows
                    total = term if total is None else total + term
            sides.append(total)
        real, imag = sides
        left_ref[0, pl.ds(first, size), :] = real.astype(BF16)
        left_ref[1, pl.ds(first, size), :] = (-imag).astype(BF16)
        left_ref[0, pl.ds(first + size, size), :] = imag.astype(BF16)
        left_ref[1, pl.ds(first + size, size), :] = real.astype(BF16)

    for at in range(sets):
        line_set(at, pl.multiple_of(starts_ref[at], size))


def interpolate(starts, offsets, taps, echo):
    pings, lines = echo.shape[1:]
    scalars = pl.BlockSpec(memory_space=pltpu.SMEM)
    return pl.pallas_call(
        interp_kernel,
        grid=(pings // LANES,),
        out_shape=jax.ShapeDtypeStruct((2, 2 * lines, pings), BF16),
        in_specs=[
            scalars,
            scalars,
            scalars,
            pl.BlockSpec((2, LANES, lines), lambda i: (0, i, 0)),
        ],
        out_specs=pl.BlockSpec((2, 2 * lines, LANES), lambda i: (0, 0, i)),
        scratch_shapes=[pltpu.VMEM((2, MARGIN + lines, LANES), F32)],
        compiler_params=pltpu.CompilerParams(vmem_limit_bytes=48 * 2**20),
        cost_estimate=pl.CostEstimate(flops=16 * pings * lines, bytes_accessed=12 * pings * lines, transcendentals=0),
        name="interp",
    )(starts, offsets, taps, echo)


def largest_kernel(echo_ref, taps_ref, steer_ref, most_ref, here_ref, sems):
    pieces, sets, rows, width = here_ref.shape
    copies = [
        pltpu.make_async_copy(steer_ref.at[:, pl.ds(at * rows, rows), :], here_ref.at[at], sems.at[at])
        for at in range(pieces)
    ]
    for copy in copies:
        copy.start()
    for at, ref in enumerate((echo_ref, taps_ref)):
        most_ref[at] = jnp.full(most_ref.shape[1:], jnp.max(jnp.abs(ref[...]).astype(F32)), F32)
    most = jnp.zeros((16, width), here_ref.dtype)
    for at, copy in enumerate(copies):
        copy.wait()
        most = jnp.maximum(most, jnp.max(jnp.abs(here_ref[at]).reshape(sets * rows // 16, 16, width), axis=0))
    most_ref[2] = jnp.full(most_ref.shape[1:], jnp.max(most.astype(F32)), F32)


def largest(echo, taps, steer):
    sets, rows, width = steer.shape
    pieces = max(1, rows // 512)
    whole = pl.BlockSpec(memory_space=pltpu.VMEM)
    return pl.pallas_call(
        largest_kernel,
        out_shape=jax.ShapeDtypeStruct((3, 8, LANES), F32),
        in_specs=[whole, whole, pl.BlockSpec(memory_space=pl.ANY)],
        out_specs=whole,
        scratch_shapes=[
            pltpu.VMEM((pieces, sets, rows // pieces, width), steer.dtype),
            pltpu.SemaphoreType.DMA((pieces,)),
        ],
        compiler_params=pltpu.CompilerParams(vmem_limit_bytes=56 * 2**20),
        cost_estimate=pl.CostEstimate(flops=steer.size, bytes_accessed=2 * steer.size, transcendentals=0),
        name="largest",
    )(echo, taps, steer)


def image_kernel(left_ref, steer_ref, mine_ref, theirs_ref):
    contract = (((1,), (1,)), ((), ()))
    half = mine_ref.shape[0]
    for rows, out_ref in ((slice(half, None), theirs_ref), (slice(0, half), mine_ref)):
        total = lax.dot_general(left_ref[0, rows, :], steer_ref[0], contract, preferred_element_type=F32)
        total = total + lax.dot_general(left_ref[1, rows, :], steer_ref[1], contract, preferred_element_type=F32)
        out_ref[...] = total


def partial_image(left, steer, first, cells):
    _, rows, pings = left.shape
    tile = math.gcd(math.gcd(first, cells), 512 if rows <= 512 else 128)
    half = rows // 2
    return pl.pallas_call(
        image_kernel,
        grid=(cells // tile,),
        out_shape=(jax.ShapeDtypeStruct((half, cells), F32),) * 2,
        in_specs=[
            pl.BlockSpec(memory_space=pltpu.VMEM),
            pl.BlockSpec((2, tile, pings), lambda i: (0, first // tile + i, 0)),
        ],
        out_specs=(pl.BlockSpec((half, tile), lambda i: (0, i)),) * 2,
        compiler_params=pltpu.CompilerParams(vmem_limit_bytes=40 * 2**20),
        cost_estimate=pl.CostEstimate(
            flops=4 * rows * cells * pings, bytes_accessed=4 * cells * pings + 8 * half * cells, transcendentals=0
        ),
        name="image",
    )(left, steer)


def split_terms(value):
    high = value.astype(BF16)
    low = (value - high.astype(F32)).astype(BF16)
    return high, low


def forward(lines_pair, over_rows_ref, over_lanes_ref, twist_ref):
    rows = lines_pair[0][0].shape[0]
    grid = jnp.concatenate([jnp.concatenate(line, axis=0) for line in lines_pair], axis=1)
    high, low = split_terms(grid)
    first = jnp.dot(
        over_rows_ref[...], jnp.concatenate([high, low, high], axis=0), preferred_element_type=F32
    )
    twisted = []
    for at in range(len(lines_pair)):
        real = first[:rows, at * LANES : (at + 1) * LANES]
        imag = first[rows:, at * LANES : (at + 1) * LANES]
        cos, sin = twist_ref[0], twist_ref[1]
        twisted.append(jnp.concatenate([real * cos - imag * sin, real * sin + imag * cos], axis=1))
    high, low = split_terms(jnp.concatenate(twisted, axis=0))
    second = jnp.dot(
        jnp.concatenate([high, low, high], axis=1), over_lanes_ref[...], preferred_element_type=F32
    )
    return [second[at * rows : (at + 1) * rows] for at in range(len(lines_pair))]


def gradient_kernel(
    count,
    cuts,
    tile_ref,
    centers_ref,
    halves_ref,
    turn_ref,
    down_ref,
    over_rows_ref,
    over_lanes_ref,
    twist_ref,
    *refs,
):
    own_refs, far_refs, (grid_ref, sums_ref) = refs[: len(cuts)], refs[len(cuts) : -2], refs[-2:]
    lines = own_refs[0].shape[0] // 2
    rows = grid_ref.shape[1] // lines
    length = rows * LANES
    down = jnp.concatenate([down_ref[...]] * (lines // 8), axis=0)
    for (start, cells), own_ref, far_ref in zip(cuts, own_refs, far_refs):
        for piece in range(count):
            source = own_ref if piece == 0 else far_ref.at[piece - 1]
            base = tile_ref[piece] * (rows // count) + start // LANES
            for row in range(cells // LANES):
                first = pl.multiple_of((base + row) * lines, lines)
                for part in range(2):
                    value = source[part * lines : (part + 1) * lines, row * LANES : (row + 1) * LANES]
                    grid_ref[part, pl.ds(first, lines), :] = value * down
    cell = lax.broadcasted_iota(jnp.int32, (rows, LANES), 0) * LANES + lax.broadcasted_iota(
        jnp.int32, (rows, LANES), 1
    )
    bottom = lax.broadcasted_iota(jnp.int32, (rows, LANES), 0) == rows - 1
    numer = jnp.zeros((rows, LANES), F32)
    denom = jnp.zeros((rows, LANES), F32)
    for pair in range(0, lines, 2):
        windowed = []
        for line in (pair, pair + 1):
            away = cell - centers_ref[line]
            away = jnp.where(away < 0, away + length, away)
            inside = jnp.minimum(away, length - away) <= halves_ref[line]
            windowed.append(
                [jnp.where(inside, grid_ref[part, pl.ds(line, rows, stride=lines), :], 0.0) for part in range(2)]
            )
        bins = forward(windowed, over_rows_ref, over_lanes_ref, twist_ref)
        for line, value in zip((pair, pair + 1), bins):
            real, imag = value[:, :LANES], value[:, LANES:]
            turned = []
            for side in (real, imag):
                up = pltpu.roll(side, rows - 1, 0)
                turned.append(jnp.where(bottom, pltpu.roll(up, LANES - 1, 1), up))
            next_real, next_imag = turned
            cross_real = real * next_real + imag * next_imag
            cross_imag = real * next_imag - imag * next_real
            numer = numer + (cross_real * turn_ref[1, line] + cross_imag * turn_ref[0, line])
            denom = denom + (real * real + imag * imag)
    sums_ref[0] = numer
    sums_ref[1] = denom


def gradient(tiles, cuts, centers, halves, turn, down, tables, own, far):
    count = tiles.shape[0]
    lines = own[0].shape[0] // 2
    length = count * sum(cells for _, cells in cuts)
    scalars = pl.BlockSpec(memory_space=pltpu.SMEM)
    whole = pl.BlockSpec(memory_space=pltpu.VMEM)
    return pl.pallas_call(
        functools.partial(gradient_kernel, count, cuts),
        out_shape=(
            jax.ShapeDtypeStruct((2, length // LANES * lines, LANES), F32),
            jax.ShapeDtypeStruct((2, length // LANES, LANES), F32),
        ),
        in_specs=[scalars] * 4 + [whole] * (4 + 2 * len(cuts)),
        out_specs=(whole, whole),
        compiler_params=pltpu.CompilerParams(vmem_limit_bytes=40 * 2**20),
        cost_estimate=pl.CostEstimate(flops=2400 * lines * length, bytes_accessed=16 * lines * length, transcendentals=0),
        name="gradient",
    )(tiles, centers, halves, turn, down, *tables, *own, *far)


def spectrum_kernel(lines, over_rows_ref, over_lanes_ref, twist_ref, grid_ref, bins_ref):
    rows = grid_ref.shape[1] // lines
    for pair in range(0, lines, 2):
        both = [
            [grid_ref[part, pl.ds(line, rows, stride=lines), :] for part in range(2)] for line in (pair, pair + 1)
        ]
        for line, value in zip((pair, pair + 1), forward(both, over_rows_ref, over_lanes_ref, twist_ref)):
            bins_ref[line * rows : (line + 1) * rows, :] = value


def spectrum(tables, grid, lines):
    whole = pl.BlockSpec(memory_space=pltpu.VMEM)
    rows = grid.shape[1] // lines
    return pl.pallas_call(
        functools.partial(spectrum_kernel, lines),
        out_shape=jax.ShapeDtypeStruct((lines * rows, 2 * LANES), F32),
        in_specs=[whole] * 4,
        out_specs=whole,
        compiler_params=pltpu.CompilerParams(vmem_limit_bytes=40 * 2**20),
        cost_estimate=pl.CostEstimate(
            flops=2400 * lines * rows * LANES, bytes_accessed=16 * lines * rows * LANES, transcendentals=0
        ),
        name="spectrum",
    )(*tables, grid)


def three_terms(value):
    high, rest = value.astype(BF16), value
    rest = value - high.astype(F32)
    middle = rest.astype(BF16)
    low = (rest - middle.astype(F32)).astype(BF16)
    return [high, middle, low]


def focus_kernel(
    over_rows_ref, over_lanes_ref, twist_ref, below_ref, across_ref, sums_ref, bins_ref, out_ref, phase_ref, grid_ref, turned_ref
):
    rows = twist_ref.shape[1]
    lines = out_ref.shape[1]
    length = rows * LANES
    slope = sums_ref[0] / (sums_ref[1] + EPSILON)
    inner = jnp.dot(below_ref[...], jnp.concatenate(three_terms(slope), axis=0), preferred_element_type=F32)
    column = inner[rows - 8 :] + slope[rows - 8 :]
    outer = jnp.dot(jnp.concatenate(three_terms(column), axis=1), across_ref[...], preferred_element_type=F32)
    prefix = inner + outer[7:8, :LANES]
    place = lax.broadcasted_iota(jnp.int32, (rows, LANES), 0) + rows * lax.broadcasted_iota(
        jnp.int32, (rows, LANES), 1
    )
    phase = prefix - place.astype(F32) * (outer[7:8, LANES:] * (1.0 / length))
    turned_ref[...] = jnp.transpose(phase)
    runs = LANES // rows
    phase_ref[...] = jnp.concatenate(
        [turned_ref[pl.ds(at, rows, stride=runs), :] for at in range(runs)], axis=1
    )
    cos, sin = jnp.cos(phase), jnp.sin(phase)
    for pair in range(0, lines, 2):
        fixed = []
        for line in (pair, pair + 1):
            real = bins_ref[line * rows : (line + 1) * rows, :LANES]
            imag = bins_ref[line * rows : (line + 1) * rows, LANES:]
            fixed.append(jnp.concatenate([real * cos + imag * sin, imag * cos - real * sin], axis=1))
        high, low = split_terms(jnp.concatenate(fixed, axis=0))
        first = jnp.dot(
            jnp.concatenate([high, low, high], axis=1), over_lanes_ref[...], preferred_element_type=F32
        )
        twisted = []
        for at in range(2):
            real = first[at * rows : (at + 1) * rows, :LANES]
            imag = first[at * rows : (at + 1) * rows, LANES:]
            turn_cos, turn_sin = twist_ref[0], twist_ref[1]
            twisted.append(
                jnp.concatenate([real * turn_cos - imag * turn_sin, real * turn_sin + imag * turn_cos], axis=0)
            )
        high, low = split_terms(jnp.concatenate(twisted, axis=1))
        second = jnp.dot(
            over_rows_ref[...], jnp.concatenate([high, low, high], axis=0), preferred_element_type=F32
        )
        for at in range(2):
            for part in range(2):
                grid_ref[part, pl.ds(pair + at, rows, stride=lines), :] = second[
                    part * rows : (part + 1) * rows, at * LANES : (at + 1) * LANES
                ]
    for row in range(rows):
        for part in range(2):
            out_ref[part, :, row * LANES : (row + 1) * LANES] = grid_ref[part, row * lines : (row + 1) * lines, :]


def focus(tables, prefix_tables, sums, bins, lines):
    whole = pl.BlockSpec(memory_space=pltpu.VMEM)
    rows = sums.shape[1]
    return pl.pallas_call(
        focus_kernel,
        out_shape=(
            jax.ShapeDtypeStruct((2, lines, rows * LANES), F32),
            jax.ShapeDtypeStruct((rows, LANES), F32),
        ),
        in_specs=[whole] * 7,
        out_specs=(whole, whole),
        scratch_shapes=[pltpu.VMEM((2, rows * lines, LANES), F32), pltpu.VMEM((LANES, rows), F32)],
        compiler_params=pltpu.CompilerParams(vmem_limit_bytes=40 * 2**20),
        cost_estimate=pl.CostEstimate(
            flops=2400 * lines * rows * LANES, bytes_accessed=16 * lines * rows * LANES, transcendentals=0
        ),
        name="focus",
    )(*tables, *prefix_tables, sums, bins)


def swap(value, axis, bit):
    count = lax.axis_size(axis)
    return lax.ppermute(value, axis, [(at, at ^ bit) for at in range(count)])


def total_over(value, pairs):
    for at in range(0, len(pairs), 2):
        (axis, bit), *more = sorted(pairs[at : at + 2])
        first = swap(value, axis, bit)
        for other, other_bit in more:
            second = swap(value, other, other_bit)
            if other == axis:
                third = swap(value, axis, bit ^ other_bit)
            else:
                count, inner = lax.axis_size(axis), lax.axis_size(other)
                both = [(i, ((i // inner) ^ bit) * inner + ((i % inner) ^ other_bit)) for i in range(count * inner)]
                third = lax.ppermute(value, (axis, other), both)
            value, first = value + first, second + third
        value = value + first
    return value


def gather_lines(value, axis):
    if lax.axis_size(axis) != 2:
        return lax.all_gather(value, axis, axis=2, tiled=True)
    other = swap(value, axis, 1)
    first = lax.axis_index(axis) == 0
    return jnp.concatenate([jnp.where(first, value, other), jnp.where(first, other, value)], axis=2)


def scale_of(known, terms):
    bound = jnp.clip(terms * known[0] * known[1] * known[2], 1e-30, 1e30)
    power = jnp.clip(jnp.floor(jnp.log2(2.0**15 / bound)), -100.0, 100.0)
    return lax.optimization_barrier((jnp.exp2(power), jnp.exp2(-power)))


def start_rows(pings, tiles, lines):
    me, tile = lax.axis_index("ping"), lax.axis_index("rng")
    owner = jnp.arange(pings * tiles, dtype=jnp.int32)
    apart = (owner // tiles) ^ me
    slot = jnp.zeros_like(apart)
    bit = 1
    while bit < pings:
        slot = 2 * slot + (apart & bit) // bit
        bit *= 2
    return (slot * tiles + (owner % tiles - tile) % tiles) * (2 * lines)


def tie(value, *others):
    return lax.optimization_barrier((value, *others))[0]


def packed(value):
    return value[value.shape[0] // 2 :].astype(SENT)


def merged(value, got):
    return value[: value.shape[0] // 2] + got.astype(F32)


def on_device(echo, steer, offsets, taps, centers, halves):
    pings = lax.axis_size("ping")
    tiles = lax.axis_size("rng")
    tile = lax.axis_index("rng")
    lines = centers.shape[0]
    length = steer.shape[1] * tiles
    cuts = cuts_of(steer.shape[1])

    echo_lines = gather_lines(echo, "rng")
    taps = taps.T
    known = largest(echo, taps, steer)
    known = jnp.maximum(known, swap(known, "ping", 1))
    bits = [1 << at for at in range(1, pings.bit_length() - 1)]
    echo_lines = tie(echo_lines, known)
    others = [swap(known, "ping", 2 * at) for at in range(1, pings // 2)]
    left = interpolate(start_rows(pings, tiles, lines), offsets, taps, echo_lines)
    known = functools.reduce(jnp.maximum, lax.optimization_barrier((known, left, *others))[2:], known)

    count = len(cuts)
    totals, moving = [None] * count, [None] * count

    def advance(at, stage, gate):
        got = moving[at] if gate is None else tie(moving[at], gate)
        totals[at] = (totals[at] + got) * up[0, 0] if stage == 0 else merged(totals[at], got)
        if stage == len(bits):
            return totals[at]
        send = packed(totals[at])
        moving[at] = swap(send, "ping", bits[stage])
        return send

    gate = known
    for turn_at in range(count + 1 + len(bits)):
        if turn_at < count:
            left = tie(left, gate)
            totals[turn_at], theirs = partial_image(left, steer, *cuts[turn_at])
            moving[turn_at] = swap(theirs, "ping", 1)
            gate = theirs
        if turn_at == 0:
            bit = 1
            while bit < tiles:
                known = jnp.maximum(known, tie(swap(known, "rng", bit), gate))
                bit *= 2
            gate = known
            up, down = scale_of(known, 2.0 * NTAP * steer.shape[2] * pings)
        for stage in STAGES:
            at = turn_at - 1 - stage
            if 0 <= at < count and stage <= len(bits):
                gate = advance(at, stage, gate)
    own, far = [], []
    for total in totals:
        own.append(total[: 2 * lines])
        pieces = []
        for step in range(1, tiles):
            send = total[2 * lines * step : 2 * lines * (step + 1)]
            pieces.append(lax.ppermute(send, "rng", [(at, (at + step) % tiles) for at in range(tiles)]))
        far.append(jnp.stack(pieces))

    angle = 2.0 * math.pi / length * centers.astype(F32)
    turn = jnp.stack([jnp.cos(angle), jnp.sin(angle)])
    owners = (tile - jnp.arange(tiles, dtype=jnp.int32)) % tiles
    tables = [jnp.asarray(table) for table in dft_tables(length, -1.0)]
    grid, sums = gradient(owners, cuts, centers, halves, turn, down, tables, own, far)
    pairs = [("ping", 1)] + [("rng", 1 << at) for at in range(tiles.bit_length() - 1)] + [("ping", bit) for bit in bits]
    sums = total_over(sums, pairs)
    bins = spectrum(tables, grid, lines)
    tables = [jnp.asarray(table) for table in dft_tables(length, 1.0)]
    prefix_tables = [jnp.asarray(table) for table in sum_tables(length)]
    focused, phase = focus(tables, prefix_tables, sums, bins, lines)
    return (focused, phase.reshape(-1))


def solution(mesh):
    in_specs = (
        P(None, ("leg", "ping"), "rng"),
        P(None, ("leg", "rng"), "ping"),
        P(("leg", "ping")),
        P(("leg", "ping"), None),
        P(("leg", "ping", "rng")),
        P(("leg", "ping", "rng")),
    )
    out_specs = (P(None, ("leg", "ping", "rng"), None), P("leg"))
    return jax.shard_map(
        on_device, mesh=mesh, in_specs=in_specs, out_specs=out_specs, check_vma=False
    )
```

```python
import functools
import math

import jax
import jax.numpy as jnp
import numpy as np
from jax import lax
from jax.experimental import pallas as pl
from jax.experimental.pallas import tpu as pltpu
from jax.sharding import PartitionSpec as P

PBLK = 64
NTAP = 4
MARGIN = 24
LANES = 128
SHARES = (8, 8, 8, 4, 4)
STAGES = (0, 1, 2)
EPSILON = 1e-06
BF16 = jnp.bfloat16
F32 = jnp.float32
SENT = jnp.float16


def cuts_of(cells):
    units, total = cells // LANES, sum(SHARES)
    sizes = [units * share // total for share in SHARES]
    if units % total:
        count = math.gcd(units, len(SHARES))
        sizes = [units // count] * count
    cuts, first = [], 0
    for size in sizes:
        cuts.append((first * LANES, size * LANES))
        first += size
    return cuts


def two_terms(table):
    high = table.astype(np.float32).astype(jnp.bfloat16)
    low = (table - high.astype(np.float64)).astype(np.float32).astype(jnp.bfloat16)
    return high, low


def dft_tables(length, direction):
    rows = length // LANES

    def waves(count, other, modulus):
        grid = np.outer(np.arange(count), np.arange(other)) % modulus
        angle = direction * 2.0 * math.pi / modulus * grid
        return np.cos(angle), np.sin(angle)

    scale = 1.0 if direction < 0 else 1.0 / length
    cos, sin = waves(rows, rows, rows)
    high, low = two_terms(scale * np.block([[cos, -sin], [sin, cos]]))
    over_rows = np.concatenate([high, high, low], axis=1)
    cos, sin = waves(LANES, LANES, LANES)
    high, low = two_terms(np.block([[cos, sin], [-sin, cos]]))
    over_lanes = np.concatenate([high, high, low], axis=0)
    cos, sin = waves(rows, LANES, length)
    twist = np.stack([cos, sin]).astype(np.float32)
    return over_rows, over_lanes, twist


def sum_tables(length):
    rows = length // LANES
    below = np.tril(np.ones((rows, rows)), -1)
    before = np.triu(np.ones((LANES, LANES)), 1)
    across = np.concatenate([before, np.ones((LANES, LANES))], axis=1)
    return (
        np.concatenate([below] * 3, axis=1).astype(jnp.bfloat16),
        np.concatenate([across] * 3, axis=0).astype(jnp.bfloat16),
    )


def interp_kernel(starts_ref, offsets_ref, taps_ref, echo_ref, left_ref, turned_ref):
    step = pl.program_id(0)
    lines = echo_ref.shape[2]
    sets = starts_ref.shape[0]
    size = lines // sets
    blocks = LANES // PBLK
    lane = lax.broadcasted_iota(jnp.int32, (size, LANES), 1)
    weights, rows_back = [], []
    for sub in range(blocks):
        block = step * blocks + sub
        here = lane // PBLK == sub
        weights.append([jnp.where(here, taps_ref[tap, block], 0.0) for tap in range(NTAP)])
        rows_back.append(MARGIN - offsets_ref[block])

    for part in range(2):
        turned_ref[part, :MARGIN, :] = jnp.zeros((MARGIN, LANES), F32)
        turned_ref[part, MARGIN:, :] = jnp.transpose(echo_ref[part].astype(F32))

    def line_set(at, first):
        sides = []
        for part in range(2):
            total = None
            for tap in range(NTAP):
                for sub in range(blocks):
                    rows = turned_ref[part, pl.ds(rows_back[sub] + (at * size - tap), size), :]
                    term = weights[sub][tap] * rows
                    total = term if total is None else total + term
            sides.append(total)
        real, imag = sides
        left_ref[0, pl.ds(first, size), :] = real.astype(BF16)
        left_ref[1, pl.ds(first, size), :] = (-imag).astype(BF16)
        left_ref[0, pl.ds(first + size, size), :] = imag.astype(BF16)
        left_ref[1, pl.ds(first + size, size), :] = real.astype(BF16)

    for at in range(sets):
        line_set(at, pl.multiple_of(starts_ref[at], size))


def interpolate(starts, offsets, taps, echo):
    pings, lines = echo.shape[1:]
    scalars = pl.BlockSpec(memory_space=pltpu.SMEM)
    return pl.pallas_call(
        interp_kernel,
        grid=(pings // LANES,),
        out_shape=jax.ShapeDtypeStruct((2, 2 * lines, pings), BF16),
        in_specs=[
            scalars,
            scalars,
            scalars,
            pl.BlockSpec((2, LANES, lines), lambda i: (0, i, 0)),
        ],
        out_specs=pl.BlockSpec((2, 2 * lines, LANES), lambda i: (0, 0, i)),
        scratch_shapes=[pltpu.VMEM((2, MARGIN + lines, LANES), F32)],
        compiler_params=pltpu.CompilerParams(vmem_limit_bytes=48 * 2**20),
        cost_estimate=pl.CostEstimate(flops=16 * pings * lines, bytes_accessed=12 * pings * lines, transcendentals=0),
        name="interp",
    )(starts, offsets, taps, echo)


def largest_kernel(echo_ref, taps_ref, steer_ref, most_ref, here_ref, sems):
    pieces, sets, rows, width = here_ref.shape
    copies = [
        pltpu.make_async_copy(steer_ref.at[:, pl.ds(at * rows, rows), :], here_ref.at[at], sems.at[at])
        for at in range(pieces)
    ]
    for copy in copies:
        copy.start()
    for at, ref in enumerate((echo_ref, taps_ref)):
        most_ref[at] = jnp.full(most_ref.shape[1:], jnp.max(jnp.abs(ref[...]).astype(F32)), F32)
    most = jnp.zeros((16, width), here_ref.dtype)
    for at, copy in enumerate(copies):
        copy.wait()
        most = jnp.maximum(most, jnp.max(jnp.abs(here_ref[at]).reshape(sets * rows // 16, 16, width), axis=0))
    most_ref[2] = jnp.full(most_ref.shape[1:], jnp.max(most.astype(F32)), F32)


def largest(echo, taps, steer):
    sets, rows, width = steer.shape
    pieces = max(1, rows // 512)
    whole = pl.BlockSpec(memory_space=pltpu.VMEM)
    return pl.pallas_call(
        largest_kernel,
        out_shape=jax.ShapeDtypeStruct((3, 8, LANES), F32),
        in_specs=[whole, whole, pl.BlockSpec(memory_space=pl.ANY)],
        out_specs=whole,
        scratch_shapes=[
            pltpu.VMEM((pieces, sets, rows // pieces, width), steer.dtype),
            pltpu.SemaphoreType.DMA((pieces,)),
        ],
        compiler_params=pltpu.CompilerParams(vmem_limit_bytes=56 * 2**20),
        cost_estimate=pl.CostEstimate(flops=steer.size, bytes_accessed=2 * steer.size, transcendentals=0),
        name="largest",
    )(echo, taps, steer)


def image_kernel(left_ref, steer_ref, mine_ref, theirs_ref):
    contract = (((1,), (1,)), ((), ()))
    half = mine_ref.shape[0]
    for rows, out_ref in ((slice(half, None), theirs_ref), (slice(0, half), mine_ref)):
        total = lax.dot_general(left_ref[0, rows, :], steer_ref[0], contract, preferred_element_type=F32)
        total = total + lax.dot_general(left_ref[1, rows, :], steer_ref[1], contract, preferred_element_type=F32)
        out_ref[...] = total


def partial_image(left, steer, first, cells):
    _, rows, pings = left.shape
    tile = math.gcd(math.gcd(first, cells), 512 if rows <= 512 else 128)
    half = rows // 2
    return pl.pallas_call(
        image_kernel,
        grid=(cells // tile,),
        out_shape=(jax.ShapeDtypeStruct((half, cells), F32),) * 2,
        in_specs=[
            pl.BlockSpec(memory_space=pltpu.VMEM),
            pl.BlockSpec((2, tile, pings), lambda i: (0, first // tile + i, 0)),
        ],
        out_specs=(pl.BlockSpec((half, tile), lambda i: (0, i)),) * 2,
        compiler_params=pltpu.CompilerParams(vmem_limit_bytes=40 * 2**20),
        cost_estimate=pl.CostEstimate(
            flops=4 * rows * cells * pings, bytes_accessed=4 * cells * pings + 8 * half * cells, transcendentals=0
        ),
        name="image",
    )(left, steer)


def split_terms(value):
    high = value.astype(BF16)
    low = (value - high.astype(F32)).astype(BF16)
    return high, low


def forward(lines_pair, over_rows_ref, over_lanes_ref, twist_ref):
    rows = lines_pair[0][0].shape[0]
    grid = jnp.concatenate([jnp.concatenate(line, axis=0) for line in lines_pair], axis=1)
    high, low = split_terms(grid)
    first = jnp.dot(
        over_rows_ref[...], jnp.concatenate([high, low, high], axis=0), preferred_element_type=F32
    )
    twisted = []
    for at in range(len(lines_pair)):
        real = first[:rows, at * LANES : (at + 1) * LANES]
        imag = first[rows:, at * LANES : (at + 1) * LANES]
        cos, sin = twist_ref[0], twist_ref[1]
        twisted.append(jnp.concatenate([real * cos - imag * sin, real * sin + imag * cos], axis=1))
    high, low = split_terms(jnp.concatenate(twisted, axis=0))
    second = jnp.dot(
        jnp.concatenate([high, low, high], axis=1), over_lanes_ref[...], preferred_element_type=F32
    )
    return [second[at * rows : (at + 1) * rows] for at in range(len(lines_pair))]


def gradient_kernel(
    count,
    cuts,
    tile_ref,
    centers_ref,
    halves_ref,
    turn_ref,
    down_ref,
    over_rows_ref,
    over_lanes_ref,
    twist_ref,
    *refs,
):
    own_refs, far_refs, (grid_ref, sums_ref) = refs[: len(cuts)], refs[len(cuts) : -2], refs[-2:]
    lines = own_refs[0].shape[0] // 2
    rows = grid_ref.shape[1] // lines
    length = rows * LANES
    down = jnp.concatenate([down_ref[...]] * (lines // 8), axis=0)
    for (start, cells), own_ref, far_ref in zip(cuts, own_refs, far_refs):
        for piece in range(count):
            source = own_ref if piece == 0 else far_ref.at[piece - 1]
            base = tile_ref[piece] * (rows // count) + start // LANES
            for row in range(cells // LANES):
                first = pl.multiple_of((base + row) * lines, lines)
                for part in range(2):
                    value = source[part * lines : (part + 1) * lines, row * LANES : (row + 1) * LANES]
                    grid_ref[part, pl.ds(first, lines), :] = value * down
    cell = lax.broadcasted_iota(jnp.int32, (rows, LANES), 0) * LANES + lax.broadcasted_iota(
        jnp.int32, (rows, LANES), 1
    )
    bottom = lax.broadcasted_iota(jnp.int32, (rows, LANES), 0) == rows - 1
    numer = jnp.zeros((rows, LANES), F32)
    denom = jnp.zeros((rows, LANES), F32)
    for pair in range(0, lines, 2):
        windowed = []
        for line in (pair, pair + 1):
            away = cell - centers_ref[line]
            away = jnp.where(away < 0, away + length, away)
            inside = jnp.minimum(away, length - away) <= halves_ref[line]
            windowed.append(
                [jnp.where(inside, grid_ref[part, pl.ds(line, rows, stride=lines), :], 0.0) for part in range(2)]
            )
        bins = forward(windowed, over_rows_ref, over_lanes_ref, twist_ref)
        for line, value in zip((pair, pair + 1), bins):
            real, imag = value[:, :LANES], value[:, LANES:]
            turned = []
            for side in (real, imag):
                up = pltpu.roll(side, rows - 1, 0)
                turned.append(jnp.where(bottom, pltpu.roll(up, LANES - 1, 1), up))
            next_real, next_imag = turned
            cross_real = real * next_real + imag * next_imag
            cross_imag = real * next_imag - imag * next_real
            numer = numer + (cross_real * turn_ref[1, line] + cross_imag * turn_ref[0, line])
            denom = denom + (real * real + imag * imag)
    sums_ref[0] = numer
    sums_ref[1] = denom


def gradient(tiles, cuts, centers, halves, turn, down, tables, own, far):
    count = tiles.shape[0]
    lines = own[0].shape[0] // 2
    length = count * sum(cells for _, cells in cuts)
    scalars = pl.BlockSpec(memory_space=pltpu.SMEM)
    whole = pl.BlockSpec(memory_space=pltpu.VMEM)
    return pl.pallas_call(
        functools.partial(gradient_kernel, count, cuts),
        out_shape=(
            jax.ShapeDtypeStruct((2, length // LANES * lines, LANES), F32),
            jax.ShapeDtypeStruct((2, length // LANES, LANES), F32),
        ),
        in_specs=[scalars] * 4 + [whole] * (4 + 2 * len(cuts)),
        out_specs=(whole, whole),
        compiler_params=pltpu.CompilerParams(vmem_limit_bytes=40 * 2**20),
        cost_estimate=pl.CostEstimate(flops=2400 * lines * length, bytes_accessed=16 * lines * length, transcendentals=0),
        name="gradient",
    )(tiles, centers, halves, turn, down, *tables, *own, *far)


def spectrum_kernel(lines, over_rows_ref, over_lanes_ref, twist_ref, grid_ref, bins_ref):
    rows = grid_ref.shape[1] // lines
    for pair in range(0, lines, 2):
        both = [
            [grid_ref[part, pl.ds(line, rows, stride=lines), :] for part in range(2)] for line in (pair, pair + 1)
        ]
        for line, value in zip((pair, pair + 1), forward(both, over_rows_ref, over_lanes_ref, twist_ref)):
            bins_ref[line * rows : (line + 1) * rows, :] = value


def spectrum(tables, grid, lines):
    whole = pl.BlockSpec(memory_space=pltpu.VMEM)
    rows = grid.shape[1] // lines
    return pl.pallas_call(
        functools.partial(spectrum_kernel, lines),
        out_shape=jax.ShapeDtypeStruct((lines * rows, 2 * LANES), F32),
        in_specs=[whole] * 4,
        out_specs=whole,
        compiler_params=pltpu.CompilerParams(vmem_limit_bytes=40 * 2**20),
        cost_estimate=pl.CostEstimate(
            flops=2400 * lines * rows * LANES, bytes_accessed=16 * lines * rows * LANES, transcendentals=0
        ),
        name="spectrum",
    )(*tables, grid)


def three_terms(value):
    high, rest = value.astype(BF16), value
    rest = value - high.astype(F32)
    middle = rest.astype(BF16)
    low = (rest - middle.astype(F32)).astype(BF16)
    return [high, middle, low]


def focus_kernel(
    over_rows_ref, over_lanes_ref, twist_ref, below_ref, across_ref, sums_ref, bins_ref, out_ref, phase_ref, grid_ref, turned_ref
):
    rows = twist_ref.shape[1]
    lines = out_ref.shape[1]
    length = rows * LANES
    slope = sums_ref[0] / (sums_ref[1] + EPSILON)
    inner = jnp.dot(below_ref[...], jnp.concatenate(three_terms(slope), axis=0), preferred_element_type=F32)
    column = inner[rows - 8 :] + slope[rows - 8 :]
    outer = jnp.dot(jnp.concatenate(three_terms(column), axis=1), across_ref[...], preferred_element_type=F32)
    prefix = inner + outer[7:8, :LANES]
    place = lax.broadcasted_iota(jnp.int32, (rows, LANES), 0) + rows * lax.broadcasted_iota(
        jnp.int32, (rows, LANES), 1
    )
    phase = prefix - place.astype(F32) * (outer[7:8, LANES:] * (1.0 / length))
    turned_ref[...] = jnp.transpose(phase)
    runs = LANES // rows
    phase_ref[...] = jnp.concatenate(
        [turned_ref[pl.ds(at, rows, stride=runs), :] for at in range(runs)], axis=1
    )
    cos, sin = jnp.cos(phase), jnp.sin(phase)
    for pair in range(0, lines, 2):
        fixed = []
        for line in (pair, pair + 1):
            real = bins_ref[line * rows : (line + 1) * rows, :LANES]
            imag = bins_ref[line * rows : (line + 1) * rows, LANES:]
            fixed.append(jnp.concatenate([real * cos + imag * sin, imag * cos - real * sin], axis=1))
        high, low = split_terms(jnp.concatenate(fixed, axis=0))
        first = jnp.dot(
            jnp.concatenate([high, low, high], axis=1), over_lanes_ref[...], preferred_element_type=F32
        )
        twisted = []
        for at in range(2):
            real = first[at * rows : (at + 1) * rows, :LANES]
            imag = first[at * rows : (at + 1) * rows, LANES:]
            turn_cos, turn_sin = twist_ref[0], twist_ref[1]
            twisted.append(
                jnp.concatenate([real * turn_cos - imag * turn_sin, real * turn_sin + imag * turn_cos], axis=0)
            )
        high, low = split_terms(jnp.concatenate(twisted, axis=1))
        second = jnp.dot(
            over_rows_ref[...], jnp.concatenate([high, low, high], axis=0), preferred_element_type=F32
        )
        for at in range(2):
            for part in range(2):
                grid_ref[part, pl.ds(pair + at, rows, stride=lines), :] = second[
                    part * rows : (part + 1) * rows, at * LANES : (at + 1) * LANES
                ]
    for row in range(rows):
        for part in range(2):
            out_ref[part, :, row * LANES : (row + 1) * LANES] = grid_ref[part, row * lines : (row + 1) * lines, :]


def focus(tables, prefix_tables, sums, bins, lines):
    whole = pl.BlockSpec(memory_space=pltpu.VMEM)
    rows = sums.shape[1]
    return pl.pallas_call(
        focus_kernel,
        out_shape=(
            jax.ShapeDtypeStruct((2, lines, rows * LANES), F32),
            jax.ShapeDtypeStruct((rows, LANES), F32),
        ),
        in_specs=[whole] * 7,
        out_specs=(whole, whole),
        scratch_shapes=[pltpu.VMEM((2, rows * lines, LANES), F32), pltpu.VMEM((LANES, rows), F32)],
        compiler_params=pltpu.CompilerParams(vmem_limit_bytes=40 * 2**20),
        cost_estimate=pl.CostEstimate(
            flops=2400 * lines * rows * LANES, bytes_accessed=16 * lines * rows * LANES, transcendentals=0
        ),
        name="focus",
    )(*tables, *prefix_tables, sums, bins)


def swap(value, axis, bit):
    count = lax.axis_size(axis)
    return lax.ppermute(value, axis, [(at, at ^ bit) for at in range(count)])


def total_over(value, pairs):
    for at in range(0, len(pairs), 2):
        (axis, bit), *more = sorted(pairs[at : at + 2])
        first = swap(value, axis, bit)
        for other, other_bit in more:
            second = swap(value, other, other_bit)
            if other == axis:
                third = swap(value, axis, bit ^ other_bit)
            else:
                count, inner = lax.axis_size(axis), lax.axis_size(other)
                both = [(i, ((i // inner) ^ bit) * inner + ((i % inner) ^ other_bit)) for i in range(count * inner)]
                third = lax.ppermute(value, (axis, other), both)
            value, first = value + first, second + third
        value = value + first
    return value


def gather_lines(value, axis):
    if lax.axis_size(axis) != 2:
        return lax.all_gather(value, axis, axis=2, tiled=True)
    other = swap(value, axis, 1)
    first = lax.axis_index(axis) == 0
    return jnp.concatenate([jnp.where(first, value, other), jnp.where(first, other, value)], axis=2)


def scale_of(known, terms):
    bound = jnp.clip(terms * known[0] * known[1] * known[2], 1e-30, 1e30)
    power = jnp.clip(jnp.floor(jnp.log2(2.0**15 / bound)), -100.0, 100.0)
    return lax.optimization_barrier((jnp.exp2(power), jnp.exp2(-power)))


def start_rows(pings, tiles, lines):
    me, tile = lax.axis_index("ping"), lax.axis_index("rng")
    owner = jnp.arange(pings * tiles, dtype=jnp.int32)
    apart = (owner // tiles) ^ me
    slot = jnp.zeros_like(apart)
    bit = 1
    while bit < pings:
        slot = 2 * slot + (apart & bit) // bit
        bit *= 2
    return (slot * tiles + (owner % tiles - tile) % tiles) * (2 * lines)


def tie(value, *others):
    return lax.optimization_barrier((value, *others))[0]


def packed(value):
    return value[value.shape[0] // 2 :].astype(SENT)


def merged(value, got):
    return value[: value.shape[0] // 2] + got.astype(F32)


def on_device(echo, steer, offsets, taps, centers, halves):
    pings = lax.axis_size("ping")
    tiles = lax.axis_size("rng")
    tile = lax.axis_index("rng")
    lines = centers.shape[0]
    length = steer.shape[1] * tiles
    cuts = cuts_of(steer.shape[1])

    echo_lines = gather_lines(echo, "rng")
    taps = taps.T
    known = largest(echo, taps, steer)
    known = jnp.maximum(known, swap(known, "ping", 1))
    bits = [1 << at for at in range(1, pings.bit_length() - 1)]
    echo_lines = tie(echo_lines, known)
    others = [swap(known, "ping", 2 * at) for at in range(1, pings // 2)]
    left = interpolate(start_rows(pings, tiles, lines), offsets, taps, echo_lines)
    known = functools.reduce(jnp.maximum, lax.optimization_barrier((known, left, *others))[2:], known)

    count = len(cuts)
    totals, moving = [None] * count, [None] * count

    def advance(at, stage, gate):
        got = moving[at] if gate is None else tie(moving[at], gate)
        totals[at] = (totals[at] + got) * up[0, 0] if stage == 0 else merged(totals[at], got)
        if stage == len(bits):
            return totals[at]
        send = packed(totals[at])
        moving[at] = swap(send, "ping", bits[stage])
        return send

    gate = known
    for turn_at in range(count + 1 + len(bits)):
        if turn_at < count:
            left = tie(left, gate)
            totals[turn_at], theirs = partial_image(left, steer, *cuts[turn_at])
            moving[turn_at] = swap(theirs, "ping", 1)
            gate = theirs
        spread = [1 << at for at in range(tiles.bit_length() - 1)]
        if turn_at < 2 and turn_at < count:
            for bit in spread[:-1] if turn_at == 0 else spread[-1:]:
                known = jnp.maximum(known, tie(swap(known, "rng", bit), gate))
            gate = tie(gate, known)
        if turn_at == 1:
            up, down = scale_of(known, 2.0 * NTAP * steer.shape[2] * pings)
        for stage in STAGES:
            at = turn_at - 1 - stage
            if 0 <= at < count and stage <= len(bits):
                gate = advance(at, stage, gate)
    own, far = [], []
    for total in totals:
        own.append(total[: 2 * lines])
        pieces = []
        for step in range(1, tiles):
            send = total[2 * lines * step : 2 * lines * (step + 1)]
            pieces.append(lax.ppermute(send, "rng", [(at, (at + step) % tiles) for at in range(tiles)]))
        far.append(jnp.stack(pieces))

    angle = 2.0 * math.pi / length * centers.astype(F32)
    turn = jnp.stack([jnp.cos(angle), jnp.sin(angle)])
    owners = (tile - jnp.arange(tiles, dtype=jnp.int32)) % tiles
    tables = [jnp.asarray(table) for table in dft_tables(length, -1.0)]
    grid, sums = gradient(owners, cuts, centers, halves, turn, down, tables, own, far)
    pairs = [("ping", 1)] + [("rng", 1 << at) for at in range(tiles.bit_length() - 1)] + [("ping", bit) for bit in bits]
    sums = total_over(sums, pairs)
    bins = spectrum(tables, grid, lines)
    tables = [jnp.asarray(table) for table in dft_tables(length, 1.0)]
    prefix_tables = [jnp.asarray(table) for table in sum_tables(length)]
    focused, phase = focus(tables, prefix_tables, sums, bins, lines)
    return (focused, phase.reshape(-1))


def solution(mesh):
    in_specs = (
        P(None, ("leg", "ping"), "rng"),
        P(None, ("leg", "rng"), "ping"),
        P(("leg", "ping")),
        P(("leg", "ping"), None),
        P(("leg", "ping", "rng")),
        P(("leg", "ping", "rng")),
    )
    out_specs = (P(None, ("leg", "ping", "rng"), None), P("leg"))
    return jax.shard_map(
        on_device, mesh=mesh, in_specs=in_specs, out_specs=out_specs, check_vma=False
    )
```
